32 devices in a mesh: row: 4 (over z), col: 8 (over y, x, core).
Axes of the slice: x: 2, y: 2, z: 4, core: 2. Of those that a mesh axis runs over, the one named last changes fastest.
Arguments:
- tokens: bfloat16 [512, 12288], P('col', 'row'), may hold values from -6 to 6
- w_in: bfloat16 [12288, 24576], P('row', 'col'), may hold values from -0.0546875 to 0.0546875
- w_out: bfloat16 [24576, 12288], P('col', 'row'), may hold values from -0.0390625 to 0.0390625
- grad_out: bfloat16 [512, 12288], P('col', 'row'), may hold values from -6 to 6
Outputs:
- out: bfloat16 [512, 12288], P('col', 'row')
- grad_tokens: bfloat16 [512, 12288], P('col', 'row')
- grad_w_in: bfloat16 [12288, 24576], P('row', 'col')
- grad_w_out: bfloat16 [24576, 12288], P('col', 'row')
The draws below stay inside these ranges and needn't reach their ends.
All inputs are finite; a program needn't handle non-finite values.
Results may differ from the reference program's by a relative error of at most 0.013.
Values may be sent and summed in bfloat16 or wider, within the bound.
No kernel may reach another device: no remote copies, remote signals or barrier semaphores. Data moves between devices by JAX's collectives and lax.ppermute only.
A program may use at most 256 MiB of HBM per device.

```python
import jax
import jax.numpy as jnp
from jax import lax

D = 12288
FF = 24576
TOKENS = 512


def levels(rng, extent, split, least, high):
    level = 1.0
    for position, parts in split:
        steps = jax.random.uniform(jax.random.fold_in(jax.random.fold_in(rng, 6), position), (parts,), jnp.float32, least / len(split), high / len(split))
        level = level * jnp.repeat(jnp.exp(steps), extent[position] // parts).reshape((-1,) + (1,) * (len(extent) - 1 - position))
    return level


def noise(key, dims, spread, limit, cuts=(), kind=jnp.bfloat16):
    level = levels(key, dims, cuts, -0.22, 0.18) if cuts else 1.0
    array = jax.random.normal(key, dims, jnp.float32) * spread * level
    return jnp.minimum(jnp.maximum(array, -limit), limit).astype(kind)


def setup_inputs(seed: int = 0) -> dict:
    splits = jax.random.split(jax.random.key(seed), 5)
    return {
        "tokens": noise(splits[0], (TOKENS, D), 1.0, 6.0, ((0, 8), (1, 4))),
        "w_in": noise(splits[1], (D, FF), D ** -0.5, 0.0546875, ((0, 4), (1, 8))),
        "w_out": noise(splits[2], (FF, D), FF ** -0.5, 0.0390625, ((0, 8), (1, 4))),
        "grad_out": noise(splits[3], (TOKENS, D), 1.0, 6.0, ((0, 8), (1, 4))),
    }


def gelu_tanh(value):
    return 0.5 * value * (1.0 + jnp.tanh(0.7978845608 * (value + 0.044715 * value * value * value)))

def reference(tokens, w_in, w_out, grad_out):
    pre = jnp.dot(tokens, w_in, preferred_element_type=jnp.float32).astype(jnp.bfloat16)
    pre_full = pre.astype(jnp.float32)
    act = gelu_tanh(pre_full).astype(jnp.bfloat16)
    out = jnp.dot(act, w_out, preferred_element_type=jnp.float32).astype(jnp.bfloat16)
    grad_act = lax.dot_general(grad_out, w_out, (((1,), (1,)), ((), ())), preferred_element_type=jnp.float32)
    _, pullback = jax.vjp(gelu_tanh, pre_full)
    grad_pre = pullback(grad_act)[0].astype(jnp.bfloat16)
    grad_tokens = lax.dot_general(grad_pre, w_in, (((1,), (1,)), ((), ())), preferred_element_type=jnp.float32).astype(jnp.bfloat16)
    grad_w_in = lax.dot_general(tokens, grad_pre, (((0,), (0,)), ((), ())), preferred_element_type=jnp.float32).astype(jnp.bfloat16)
    grad_w_out = lax.dot_general(act, grad_out, (((0,), (0,)), ((), ())), preferred_element_type=jnp.float32).astype(jnp.bfloat16)
    return (out, grad_tokens, grad_w_in, grad_w_out)
```

```python
import jax
import jax.numpy as jnp
from jax import lax
from jax.experimental import pallas as pl
from jax.experimental.pallas import tpu as pltpu
from jax.sharding import PartitionSpec as P

BF16 = jnp.bfloat16
F32 = jnp.float32


def gelu_tanh(value):
    return 0.5 * value * (1.0 + jnp.tanh(0.7978845608 * (value + 0.044715 * value * value * value)))


def dot(left, right, left_dim, right_dim, dtype=F32):
    return lax.dot_general(
        left, right, (((left_dim,), (right_dim,)), ((), ())), preferred_element_type=F32
    ).astype(dtype)


def swap(size, bit):
    return [(i, i ^ bit) for i in range(size)]


def gather_col(block, size):
    rows = block.shape[0]
    own = jnp.concatenate([block, lax.ppermute(block, "col", swap(size, 1))])
    if size == 8:
        half = rows // 2
        by_x = lax.ppermute(block, "col", swap(size, 2))
        by_y = lax.ppermute(block, "col", swap(size, 4))
        first = lax.ppermute(by_x[:half], "col", swap(size, 4))
        second = lax.ppermute(by_y[half:], "col", swap(size, 2))
        far = jnp.concatenate([by_x, by_y, first, second])
        other = lax.ppermute(far, "col", swap(size, 1))
        rest = []
        for i in range(3):
            rest += [far[i * rows : (i + 1) * rows], other[i * rows : (i + 1) * rows]]
        return own, jnp.concatenate(rest)
    rest, whole, bit = [], own, 2
    while bit < size:
        new = lax.ppermute(whole, "col", swap(size, bit))
        rest.append(new)
        whole = jnp.concatenate([whole, new])
        bit *= 2
    return own, jnp.concatenate(rest)


def scatter_col(blocks, size):
    order = [1] + [b for b in (4, 2) if b < size] + [1 << k for k in range(3, 10) if (1 << k) < size]
    keep = dict(blocks)
    for bit in order:
        send = sorted(r for r in keep if r & bit)
        stay = [r ^ bit for r in send]
        got = lax.ppermute(jnp.concatenate([keep[r] for r in send]), "col", swap(size, bit))
        rows = got.shape[0] // len(send)
        keep = {
            r: (keep[r].astype(F32) + got[i * rows : (i + 1) * rows].astype(F32)).astype(BF16)
            for i, r in enumerate(stay)
        }
    return keep[0]


def to_middle(term, size):
    mid = size // 2 - 1
    for j in range(mid):
        term = term + lax.ppermute(term, "row", [(j, j + 1), (size - 1 - j, size - 2 - j)])
    other = lax.ppermute(term, "row", [(mid, mid + 1), (mid + 1, mid)])
    return term.astype(F32) + other.astype(F32)


def from_middle(value, size, distance):
    mid = size // 2 - 1
    for j in range(mid):
        got = lax.ppermute(
            value, "row", [(mid - j, mid - j - 1), (mid + 1 + j, mid + 2 + j)]
        )
        value = jnp.where(distance == j + 1, got, value)
    return value


def general(rows_n, cols_n):
    def on_device(tokens, w_in, w_out, grad_out):
        me = lax.axis_index("row")
        mid = rows_n // 2 - 1
        distance = jnp.where(me <= mid, mid - me, me - mid - 1)
        hidden = w_in.shape[1]
        block = tokens.shape[0]
        x_own, x_rest = gather_col(tokens, cols_n)
        dy_own, dy_rest = gather_col(grad_out, cols_n)

        def cuts(parts):
            step = hidden // parts
            return [slice(i * step, (i + 1) * step) for i in range(parts)]

        own_cuts, rest_cuts = cuts(4), cuts(6)

        def forward(x, cut):
            pre = to_middle(dot(x, w_in[:, cut], 1, 0, BF16), rows_n).astype(BF16)
            act = gelu_tanh(pre.astype(F32)).astype(BF16)
            return pre, from_middle(act, rows_n, distance)

        def backward(dy, cut, pre):
            grad_act = to_middle(dot(dy, w_out[cut, :], 1, 1, BF16), rows_n)
            _, pullback = jax.vjp(gelu_tanh, pre.astype(F32))
            return from_middle(pullback(grad_act)[0].astype(BF16), rows_n, distance)

        own_f = [forward(x_own, c) for c in own_cuts]
        rest_f = [forward(x_rest, c) for c in rest_cuts]
        rest_b = [backward(dy_rest, c, f[0]) for c, f in zip(rest_cuts, rest_f)]
        own_b = [backward(dy_own, c, f[0]) for c, f in zip(own_cuts, own_f)]

        act_own = jnp.concatenate([f[1] for f in own_f], axis=1)
        act_rest = jnp.concatenate([f[1] for f in rest_f], axis=1)
        dz_rest = jnp.concatenate(rest_b, axis=1)
        dz_own = jnp.concatenate(own_b, axis=1)
        act = jnp.concatenate([act_own, act_rest])
        dz = jnp.concatenate([dz_own, dz_rest])
        x = jnp.concatenate([x_own, x_rest])
        dy = jnp.concatenate([dy_own, dy_rest])

        def split(own, rest):
            whole = {i: own[i * block : (i + 1) * block] for i in range(2)}
            for i in range(2, cols_n):
                whole[i] = rest[(i - 2) * block : (i - 1) * block]
            return whole

        out = scatter_col(
            split(dot(act_own, w_out, 1, 0, BF16), dot(act_rest, w_out, 1, 0, BF16)), cols_n
        )
        grad_tokens = scatter_col(
            split(dot(dz_own, w_in, 1, 1, BF16), dot(dz_rest, w_in, 1, 1, BF16)), cols_n
        )
        grad_w_out = dot(act, dy, 0, 0, BF16)
        grad_w_in = dot(x, dz, 0, 0, BF16)
        return out, grad_tokens, grad_w_in, grad_w_out

    return on_device


def stack(value, parts):
    return jnp.concatenate(jnp.split(value, parts, axis=1))


def unstack(value, parts):
    return jnp.concatenate(jnp.split(value, parts), axis=1)


class Order:
    def __init__(self):
        self.last = ()
        self.open = []

    def run(self, fn, *args):
        upto = [i for i, sent in enumerate(self.open) if any(sent is arg for arg in args)]
        waits = self.open[: upto[-1] + 1] if upto else []
        self.open = self.open[len(waits) :]
        first = args[0]
        held = lax.optimization_barrier((first, self.last, waits))
        done = {id(sent): value for sent, value in zip(waits, held[2])}
        self.last = fn(held[0], *[done.get(id(arg), arg) for arg in args[1:]])
        return self.last

    def wait(self, *args):
        return self.run(lambda *values: values, *args)

    def send(self, value, axis, pairs):
        value = lax.optimization_barrier((value, self.last))[0]
        got = lax.ppermute(value, axis, pairs)
        self.open.append(got)
        return got


def call(kernel, grid, ins, outs, alias=None):
    specs = [
        pl.BlockSpec(memory_space=pl.ANY) if block is None else pl.BlockSpec(block, index)
        for _, block, index in ins
    ]
    return pl.pallas_call(
        kernel,
        grid=(grid,),
        in_specs=specs,
        out_specs=[pl.BlockSpec(block, index) for _, block, index in outs],
        out_shape=[jax.ShapeDtypeStruct(shape, BF16) for shape, _, _ in outs],
        input_output_aliases=alias or {},
        compiler_params=pltpu.CompilerParams(vmem_limit_bytes=47 * 2**20),
        cost_estimate=pl.CostEstimate(flops=1, bytes_accessed=1, transcendentals=0),
    )(*[array for array, _, _ in ins])


def whole(array):
    return array, array.shape, lambda j: (0, 0)


def product_pieces(left, rows, weight, first, pieces, size, transposed):
    dim = 1 if transposed else 0

    def kernel(l_ref, w_ref, *outs):
        j = pl.program_id(0)
        result = dot(l_ref[rows, :], w_ref[...], 1, dim, BF16)
        for i, out in enumerate(outs):

            @pl.when(j == i)
            def _():
                out[...] = result

    if transposed:
        w = (weight, (size, weight.shape[1]), lambda j: (first + j, 0))
    else:
        w = (weight, (weight.shape[0], size), lambda j: (0, first + j))
    shape = (rows.stop - rows.start, size)
    return call(kernel, pieces, [whole(left), w], [(shape, shape, lambda j: (0, 0))] * pieces)


def product_stacked(left, rows, weight, first, pieces, size, transposed):
    dim = 1 if transposed else 0

    def kernel(l_ref, w_ref, out):
        out[...] = dot(l_ref[rows, :], w_ref[...], 1, dim, BF16)

    if transposed:
        w = (weight, (size, weight.shape[1]), lambda j: (first + j, 0))
    else:
        w = (weight, (weight.shape[0], size), lambda j: (0, first + j))
    count = rows.stop - rows.start
    out = ((pieces * count, size), (count, size), lambda j: (j, 0))
    return call(kernel, pieces, [whole(left), w], [out])[0]


def product_wide(left, weight, first, tiles, size):
    def kernel(l_ref, w_ref, out):
        out[...] = dot(l_ref[...], w_ref[...], 1, 0, BF16)

    w = (weight, (weight.shape[0], size), lambda j: (0, first + j))
    out = ((left.shape[0], tiles * size), (left.shape[0], size), lambda j: (0, j))
    return call(kernel, tiles, [whole(left), w], [out])[0]


def product_back(left, rows, weight, part, parts, size, before=None):
    deep = weight.shape[1] // parts
    count = rows.stop - rows.start

    def kernel(l_ref, w_ref, *refs):
        total = dot(l_ref[rows, :], w_ref[...], 1, 1)
        if before is not None:
            total = total + refs[0][...].astype(F32)
        refs[-1][...] = total.astype(BF16)

    ins = [
        (left, (left.shape[0], deep), lambda j: (0, part)),
        (weight, (size, deep), lambda j: (j, part)),
    ]
    if before is not None:
        ins.append((before, (count, size), lambda j: (0, j)))
    out = ((count, weight.shape[0]), (count, size), lambda j: (0, j))
    return call(kernel, weight.shape[0] // size, ins, [out])[0]


def grad_kernel(left, right, *refs):
    refs[-1][...] = dot(left[...], right[...], 0, 0, BF16)


def grad_rows(left, right, part, parts, buffer=None):
    tokens, wide = left.shape
    size, tile = wide // parts, right.shape[1] // 3
    ins = [
        (left, (tokens, size), lambda j: (0, part)),
        (right, (tokens, tile), lambda j: (0, j)),
    ]
    if buffer is not None:
        ins.append((buffer, None, None))
    out = ((wide, right.shape[1]), (size, tile), lambda j: (part, j))
    return call(grad_kernel, 3, ins, [out], None if buffer is None else {2: 0})[0]


def grad_columns(left, right, part, parts, buffer=None):
    tokens, wide = left.shape
    size, tile = right.shape[1] // parts, wide // 6
    ins = [
        (left, (tokens, tile), lambda j: (0, j)),
        (right, (tokens, size), lambda j: (0, part)),
    ]
    if buffer is not None:
        ins.append((buffer, None, None))
    out = ((wide, right.shape[1]), (tile, size), lambda j: (j, part))
    return call(grad_kernel, 6, ins, [out], None if buffer is None else {2: 0})[0]


CORE, X, Y = 1, 2, 4
EVEN = [(0, 1), (1, 0), (2, 3), (3, 2)]
ODD = [(1, 2), (2, 1), (0, 0), (3, 3)]


def pipelined(tokens, w_in, w_out, grad_out):
    me = lax.axis_index("row")
    edge = (me == 0) | (me == 3)
    block, hidden = tokens.shape[0], w_in.shape[1]
    near, far = 2 * block, 6 * block
    size, count = hidden // 6, 16
    order = Order()

    def across(value, bit):
        return order.send(value, "col", swap(8, bit))

    def first_hops(value):
        return across(value, CORE), across(value, X), across(value, Y)

    def second_hops(by_x, by_y):
        return across(by_x[: block // 2], Y), across(by_y[block // 2 :], X)

    def cut(part):
        return slice(part * size, (part + 1) * size)

    def half(part):
        return slice(part * 3 * size, (part + 1) * 3 * size)

    x_core, x_x, x_y = first_hops(tokens)
    x_own = order.run(lambda a, b: jnp.concatenate([a, b]), tokens, x_core)
    terms, sums, pres, sent = {}, {}, {}, {}
    even, odd = {}, {}
    act, dz = jnp.zeros((8 * block, hidden), BF16), jnp.zeros((8 * block, hidden), BF16)
    state = {}

    def forward_own(part):
        terms[part] = order.run(
            lambda x: product_stacked(x, slice(0, near), w_in, 3 * part, 3, size, False), x_own
        )

    def forward_rest(part):
        for i, term in enumerate(
            order.run(
                lambda x: product_pieces(x, slice(near, near + far), w_in, part, 2, size, False),
                state["x"],
            )
        ):
            terms[2 + part + i] = term

    def backward_rest(part):
        for i, term in enumerate(
            order.run(
                lambda dy: product_pieces(dy, slice(near, near + far), w_out, part, 2, size, True),
                state["dy"],
            )
        ):
            terms[8 + part + i] = term

    def backward_own(part):
        terms[14 + part] = order.run(
            lambda dy: product_stacked(dy, slice(0, near), w_out, 3 * part, 3, size, True),
            state["dy"],
        )

    def store(target, item, value):
        if item < 2:
            return lax.dynamic_update_slice(target, unstack(value, 3), (0, item * 3 * size))
        return lax.dynamic_update_slice(target, value, (near, (item - 2) * size))

    def step(t):
        got, mid = even.pop(t - 2, None), odd.pop(t - 2, None)
        i, term = t - 4, terms.get(t)
        args, old = {}, None
        if got is not None:
            args["got"] = got
        if mid is not None:
            args["mid"], args["mine"] = mid, sums[i]
            if i >= 8:
                old = pres[i - 6 if i < 14 else i - 14]
        if term is not None:
            args["term"] = term
        if 0 <= t - 2 < count:
            args["own"] = terms[t - 2]
        if 0 <= t - 6 < count:
            args["sent"] = sent[t - 2]
        names = list(args)

        def work(*values):
            v, r = dict(zip(names, values)), {}
            if "own" in v:
                r["sum"] = v["got"] + v["own"]
            if "mid" in v:
                total = v["mine"].astype(F32) + v["mid"].astype(F32)
                if i < 8:
                    r["pre"] = total.astype(BF16)
                    out = gelu_tanh(r["pre"].astype(F32)).astype(BF16)
                else:
                    _, pullback = jax.vjp(gelu_tanh, old.astype(F32))
                    out = pullback(total)[0].astype(BF16)
                r["send"] = jnp.where(edge, v["term"], out) if "term" in v else out
            elif "term" in v:
                r["send"] = v["term"]
            return r

        r = order.run(work, *args.values())
        if "send" in r:
            sent[t] = r["send"]
            even[t] = order.send(r["send"], "row", EVEN)
        if "sum" in r:
            sums[t - 2] = r["sum"]
            odd[t] = order.send(r["sum"], "row", ODD)
        if "pre" in r:
            pres[i] = r["pre"]
        item = t - 6
        if "sent" in args:
            nonlocal act, dz
            target = act if item < 8 else dz
            where = item if item < 8 else item - 6 if item < 14 else item - 14

            def keep(value):
                return store(target, where, jnp.where(edge, got, value))

            new = order.run(keep, args["sent"])
            if item < 8:
                act = new
            else:
                dz = new

    def out_columns(part):
        state["out", part] = order.run(lambda a: product_wide(a, w_out, 2 * part, 2, size), act)

    def tokens_rest(part):
        state["tok"] = order.run(
            lambda d: product_back(
                d, slice(near, near + far), w_in, part, 2, size, state.get("tok")
            ),
            dz,
        )

    def tokens_own(part):
        state["own"] = order.run(
            lambda d: product_back(d, slice(0, near), w_in, part, 2, size, state.get("own")), dz
        )

    def add(a, b):
        return (a.astype(F32) + b.astype(F32)).astype(BF16)

    def scatter_start(rest):
        across_core = across(rest[3 * block :], CORE)
        return rest[: 3 * block], across_core

    def scatter_first(keep, got):
        total = order.run(lambda g, k: add(g, k), got, keep)
        wide = total.shape[1] // 2
        left, right = total[:, :wide], total[:, wide:]
        to_y = across(left[block:], Y)
        to_x = across(jnp.concatenate([right[:block], right[2 * block :]]), X)
        return left, right, to_y, to_x

    def scatter_second(left, right, from_y, from_x):
        over_x, over_y = order.run(
            lambda fy, fx: (add(fy[block:], left[:block]), add(fx[block:], right[block : 2 * block])),
            from_y,
            from_x,
        )
        return from_y[:block], from_x[:block], across(over_x, X), across(over_y, Y)

    def scatter_end(own, got_core, left0, right0, left1, right1):
        def total(g, o, l0, r0, l1, r1):
            both = jnp.concatenate(
                [l0.astype(F32) + l1.astype(F32), r0.astype(F32) + r1.astype(F32)], axis=1
            )
            return (o.astype(F32) + g.astype(F32) + both).astype(BF16)

        return order.run(total, got_core, own, left0, right0, left1, right1)

    def line_up(d, a, b, c):
        return jnp.concatenate([a, b, c, d])

    forward_own(0)
    step(0)
    x_x, x_y = order.wait(x_x, x_y)
    x_a, x_b = second_hops(x_x, x_y)
    forward_own(1)
    x_far = order.run(line_up, x_b, x_x, x_y, x_a)
    x_other = across(x_far, CORE)
    sums[0] = order.run(lambda a, b: a + b, even.pop(0), terms[0])
    step(1)
    dy_core, dy_x, dy_y = first_hops(grad_out)
    odd[2] = order.send(sums[0], "row", ODD)
    state["x"] = order.run(line_up, x_other, tokens, x_core, x_far)
    forward_rest(0)
    sent[2] = terms[2]
    even[2] = order.send(terms[2], "row", EVEN)
    dy_x, dy_y = order.wait(dy_x, dy_y)
    dy_a, dy_b = second_hops(dy_x, dy_y)
    step(3)
    forward_rest(2)
    dy_far = order.run(line_up, dy_b, dy_x, dy_y, dy_a)
    dy_other = across(dy_far, CORE)
    step(4)
    state["dy"] = order.run(line_up, dy_other, grad_out, dy_core, dy_far)
    step(5)
    forward_rest(4)
    step(6)
    backward_rest(0)
    step(7)
    step(8)
    backward_rest(2)
    step(9)
    step(10)
    backward_rest(4)
    step(11)
    backward_own(0)
    step(12)
    backward_own(1)
    step(13)
    dy = state["dy"]
    grad_w_out = None
    for part in range(3):
        grad_w_out = order.run(
            lambda a: grad_rows(a, dy, part, 3, grad_w_out), act
        )
        step(14 + part)
    for part in range(3):
        out_columns(part)
        step(17 + part)
        if part == 1:
            tokens_rest(0)
    out = order.run(
        lambda a, b, c: jnp.concatenate([a, b, c], axis=1), state["out", 0], state["out", 1], state["out", 2]
    )
    out_core = across(out[block:near], CORE)
    out_keep, out_got = scatter_start(out[near:])
    tokens_rest(1)
    tok = state["tok"]
    tok_keep, tok_got = scatter_start(tok)
    out_parts = scatter_first(out_keep, out_got)
    tok_parts = scatter_first(tok_keep, tok_got)
    step(20)
    tokens_own(0)
    x = state["x"]
    grad_w_in = order.run(lambda d: grad_columns(x, d, 0, 2), dz)
    out_l0, out_r0, out_l1, out_r1 = scatter_second(*out_parts)
    tok_l0, tok_r0, tok_l1, tok_r1 = scatter_second(*tok_parts)
    step(21)
    tokens_own(1)
    tok_own = state["own"]
    tok_core = across(tok_own[block:], CORE)
    grad_w_in = order.run(lambda d: grad_columns(x, d, 1, 2, grad_w_in), dz)
    out = scatter_end(out[:block], out_core, out_l0, out_r0, out_l1, out_r1)
    grad_tokens = scatter_end(tok_own[:block], tok_core, tok_l0, tok_r0, tok_l1, tok_r1)
    return out, grad_tokens, grad_w_in, grad_w_out


def solution(mesh):
    rows, cols = mesh.shape["row"], mesh.shape["col"]
    return jax.shard_map(
        pipelined if (rows, cols) == (4, 8) else general(rows, cols),
        mesh=mesh,
        in_specs=(P("col", "row"), P("row", "col"), P("col", "row"), P("col", "row")),
        out_specs=(P("col", "row"), P("col", "row"), P("row", "col"), P("col", "row")),
        check_vma=False,
    )
```

```python
import jax
import jax.numpy as jnp
from jax import lax
from jax.experimental import pallas as pl
from jax.experimental.pallas import tpu as pltpu
from jax.sharding import PartitionSpec as P

BF16 = jnp.bfloat16
F32 = jnp.float32


def gelu_tanh(value):
    return 0.5 * value * (1.0 + jnp.tanh(0.7978845608 * (value + 0.044715 * value * value * value)))


def dot(left, right, left_dim, right_dim, dtype=F32):
    return lax.dot_general(
        left, right, (((left_dim,), (right_dim,)), ((), ())), preferred_element_type=F32
    ).astype(dtype)


def swap(size, bit):
    return [(i, i ^ bit) for i in range(size)]


def gather_col(block, size):
    rows = block.shape[0]
    own = jnp.concatenate([block, lax.ppermute(block, "col", swap(size, 1))])
    if size == 8:
        half = rows // 2
        by_x = lax.ppermute(block, "col", swap(size, 2))
        by_y = lax.ppermute(block, "col", swap(size, 4))
        first = lax.ppermute(by_x[:half], "col", swap(size, 4))
        second = lax.ppermute(by_y[half:], "col", swap(size, 2))
        far = jnp.concatenate([by_x, by_y, first, second])
        other = lax.ppermute(far, "col", swap(size, 1))
        rest = []
        for i in range(3):
            rest += [far[i * rows : (i + 1) * rows], other[i * rows : (i + 1) * rows]]
        return own, jnp.concatenate(rest)
    rest, whole, bit = [], own, 2
    while bit < size:
        new = lax.ppermute(whole, "col", swap(size, bit))
        rest.append(new)
        whole = jnp.concatenate([whole, new])
        bit *= 2
    return own, jnp.concatenate(rest)


def scatter_col(blocks, size):
    order = [1] + [b for b in (4, 2) if b < size] + [1 << k for k in range(3, 10) if (1 << k) < size]
    keep = dict(blocks)
    for bit in order:
        send = sorted(r for r in keep if r & bit)
        stay = [r ^ bit for r in send]
        got = lax.ppermute(jnp.concatenate([keep[r] for r in send]), "col", swap(size, bit))
        rows = got.shape[0] // len(send)
        keep = {
            r: (keep[r].astype(F32) + got[i * rows : (i + 1) * rows].astype(F32)).astype(BF16)
            for i, r in enumerate(stay)
        }
    return keep[0]


def to_middle(term, size):
    mid = size // 2 - 1
    for j in range(mid):
        term = term + lax.ppermute(term, "row", [(j, j + 1), (size - 1 - j, size - 2 - j)])
    other = lax.ppermute(term, "row", [(mid, mid + 1), (mid + 1, mid)])
    return term.astype(F32) + other.astype(F32)


def from_middle(value, size, distance):
    mid = size // 2 - 1
    for j in range(mid):
        got = lax.ppermute(
            value, "row", [(mid - j, mid - j - 1), (mid + 1 + j, mid + 2 + j)]
        )
        value = jnp.where(distance == j + 1, got, value)
    return value


def general(rows_n, cols_n):
    def on_device(tokens, w_in, w_out, grad_out):
        me = lax.axis_index("row")
        mid = rows_n // 2 - 1
        distance = jnp.where(me <= mid, mid - me, me - mid - 1)
        hidden = w_in.shape[1]
        block = tokens.shape[0]
        x_own, x_rest = gather_col(tokens, cols_n)
        dy_own, dy_rest = gather_col(grad_out, cols_n)

        def cuts(parts):
            step = hidden // parts
            return [slice(i * step, (i + 1) * step) for i in range(parts)]

        own_cuts, rest_cuts = cuts(4), cuts(6)

        def forward(x, cut):
            pre = to_middle(dot(x, w_in[:, cut], 1, 0, BF16), rows_n).astype(BF16)
            act = gelu_tanh(pre.astype(F32)).astype(BF16)
            return pre, from_middle(act, rows_n, distance)

        def backward(dy, cut, pre):
            grad_act = to_middle(dot(dy, w_out[cut, :], 1, 1, BF16), rows_n)
            _, pullback = jax.vjp(gelu_tanh, pre.astype(F32))
            return from_middle(pullback(grad_act)[0].astype(BF16), rows_n, distance)

        own_f = [forward(x_own, c) for c in own_cuts]
        rest_f = [forward(x_rest, c) for c in rest_cuts]
        rest_b = [backward(dy_rest, c, f[0]) for c, f in zip(rest_cuts, rest_f)]
        own_b = [backward(dy_own, c, f[0]) for c, f in zip(own_cuts, own_f)]

        act_own = jnp.concatenate([f[1] for f in own_f], axis=1)
        act_rest = jnp.concatenate([f[1] for f in rest_f], axis=1)
        dz_rest = jnp.concatenate(rest_b, axis=1)
        dz_own = jnp.concatenate(own_b, axis=1)
        act = jnp.concatenate([act_own, act_rest])
        dz = jnp.concatenate([dz_own, dz_rest])
        x = jnp.concatenate([x_own, x_rest])
        dy = jnp.concatenate([dy_own, dy_rest])

        def split(own, rest):
            whole = {i: own[i * block : (i + 1) * block] for i in range(2)}
            for i in range(2, cols_n):
                whole[i] = rest[(i - 2) * block : (i - 1) * block]
            return whole

        out = scatter_col(
            split(dot(act_own, w_out, 1, 0, BF16), dot(act_rest, w_out, 1, 0, BF16)), cols_n
        )
        grad_tokens = scatter_col(
            split(dot(dz_own, w_in, 1, 1, BF16), dot(dz_rest, w_in, 1, 1, BF16)), cols_n
        )
        grad_w_out = dot(act, dy, 0, 0, BF16)
        grad_w_in = dot(x, dz, 0, 0, BF16)
        return out, grad_tokens, grad_w_in, grad_w_out

    return on_device


def stack(value, parts):
    return jnp.concatenate(jnp.split(value, parts, axis=1))


def unstack(value, parts):
    return jnp.concatenate(jnp.split(value, parts), axis=1)


class Order:
    def __init__(self):
        self.last = ()
        self.open = []

    def run(self, fn, *args):
        upto = [i for i, sent in enumerate(self.open) if any(sent is arg for arg in args)]
        waits = self.open[: upto[-1] + 1] if upto else []
        self.open = self.open[len(waits) :]
        first = args[0]
        held = lax.optimization_barrier((first, self.last, waits))
        done = {id(sent): value for sent, value in zip(waits, held[2])}
        self.last = fn(held[0], *[done.get(id(arg), arg) for arg in args[1:]])
        return self.last

    def wait(self, *args):
        return self.run(lambda *values: values, *args)

    def send(self, value, axis, pairs):
        value = lax.optimization_barrier((value, self.last))[0]
        got = lax.ppermute(value, axis, pairs)
        self.open.append(got)
        return got


HINTS = [10, 10, 10, 10, 10, 10, 10, 10, 10, 10, 10, 10, 10, 10, 10, 10, 10, 10, 10, 10, 10, 10, 10, 10, 10]
CALLS = [0]


def call(kernel, grid, ins, outs, alias=None, scratch=()):
    CALLS[0] += 1
    specs = [
        pl.BlockSpec(memory_space=pl.ANY) if block is None else pl.BlockSpec(block, index)
        for _, block, index in ins
    ]
    return pl.pallas_call(
        kernel,
        grid=(grid,),
        in_specs=specs,
        out_specs=[pl.BlockSpec(block, index) for _, block, index in outs],
        out_shape=[jax.ShapeDtypeStruct(shape, BF16) for shape, _, _ in outs],
        scratch_shapes=list(scratch),
        input_output_aliases=alias or {},
        compiler_params=pltpu.CompilerParams(vmem_limit_bytes=43 * 2**20),
        cost_estimate=pl.CostEstimate(flops=int(1e8 * HINTS[CALLS[0] % len(HINTS)]), bytes_accessed=1, transcendentals=0),
    )(*[array for array, _, _ in ins])


def whole(array):
    return array, array.shape, lambda j: (0, 0)


def weight_slices(weight, first, size, transposed):
    if transposed:
        return weight, (size, weight.shape[1]), lambda j: (first + j, 0)
    return weight, (weight.shape[0], size), lambda j: (0, first + j)


def product_pieces(left, rows, weight, first, pieces, size, transposed):
    dim = 1 if transposed else 0
    blocks = left if isinstance(left, list) else []

    def kernel(*refs):
        j = pl.program_id(0)
        if blocks:
            parts, w_ref, l_ref, outs = refs[: len(blocks)], *refs[len(blocks) :][:2], refs[len(blocks) + 2 :]

            @pl.when(j == 0)
            def _():
                for i, part in enumerate(parts):
                    l_ref[i * part.shape[0] : (i + 1) * part.shape[0], :] = part[...]

        else:
            l_ref, w_ref, outs = refs[0], refs[1], refs[2:]
        result = dot(l_ref[rows, :], w_ref[...], 1, dim, BF16)
        for i, out in enumerate(outs):

            @pl.when(j == i)
            def _():
                out[...] = result

    shape = (rows.stop - rows.start, size)
    outs = [(shape, shape, lambda j: (0, 0))] * pieces
    ins = [whole(array) for array in blocks or [left]]
    if blocks:
        joined = (sum(array.shape[0] for array in blocks), blocks[0].shape[1])
        outs = [(joined, joined, lambda j: (0, 0))] + outs
    return call(kernel, pieces, ins + [weight_slices(weight, first, size, transposed)], outs)


def product_own(blocks, weight, first, halves, size, transposed):
    rows, wide = sum(array.shape[0] for array in blocks), blocks[0].shape[1]

    def kernel(*refs):
        j = pl.program_id(0)
        parts, w_ref = refs[: len(blocks)], refs[len(blocks)]
        outs, joined = refs[len(blocks) + 1 : -1], refs[-1]

        @pl.when(j == 0)
        def _():
            for i, part in enumerate(parts):
                joined[i * part.shape[0] : (i + 1) * part.shape[0], :] = part[...]

        if transposed:
            result = dot(w_ref[...], joined[...], 1, 1).T.astype(BF16)
        else:
            result = dot(joined[...], w_ref[...], 1, 0, BF16)
        for i in range(3 * halves):

            @pl.when(j == i)
            def _():
                outs[i // 3][(i % 3) * rows : (i % 3 + 1) * rows, :] = result

    shape = (3 * rows, size)
    return call(
        kernel,
        3 * halves,
        [whole(array) for array in blocks] + [weight_slices(weight, first, size, transposed)],
        [(shape, shape, lambda j: (0, 0))] * halves,
        scratch=[pltpu.VMEM((rows, wide), BF16)],
    )


def product_wide(left, weight, first, tiles, size):
    def kernel(l_ref, w_ref, out):
        out[...] = dot(l_ref[...], w_ref[...], 1, 0, BF16)

    w = (weight, (weight.shape[0], size), lambda j: (0, first + j))
    out = ((left.shape[0], tiles * size), (left.shape[0], size), lambda j: (0, j))
    return call(kernel, tiles, [whole(left), w], [out])[0]


def product_back(left, rows, weight, part, parts, size, before=None):
    deep = weight.shape[1] // parts
    count = rows.stop - rows.start

    def kernel(l_ref, w_ref, *refs):
        if count <= 128:
            total = dot(w_ref[...], l_ref[rows, :], 1, 1).T
        else:
            total = dot(l_ref[rows, :], w_ref[...], 1, 1)
        if before is not None:
            total = total + refs[0][...].astype(F32)
        refs[-1][...] = total.astype(BF16)

    ins = [
        (left, (left.shape[0], deep), lambda j: (0, part)),
        (weight, (size, deep), lambda j: (j, part)),
    ]
    if before is not None:
        ins.append((before, (count, size), lambda j: (0, j)))
    out = ((count, weight.shape[0]), (count, size), lambda j: (0, j))
    return call(kernel, weight.shape[0] // size, ins, [out])[0]


def grad_kernel(left, right, *refs):
    refs[-1][...] = dot(left[...], right[...], 0, 0, BF16)


def grad_rows(left, right, part, parts, buffer=None):
    tokens, wide = left.shape
    size, tile = wide // parts, right.shape[1] // 3
    ins = [
        (left, (tokens, size), lambda j: (0, part)),
        (right, (tokens, tile), lambda j: (0, j)),
    ]
    if buffer is not None:
        ins.append((buffer, None, None))
    out = ((wide, right.shape[1]), (size, tile), lambda j: (part, j))
    return call(grad_kernel, 3, ins, [out], None if buffer is None else {2: 0})[0]


def grad_columns(left, right, part, parts, buffer=None):
    tokens, wide = left.shape
    size, tile = right.shape[1] // parts, wide // 3
    ins = [
        (left, (tokens, tile), lambda j: (0, j)),
        (right, (tokens, size), lambda j: (0, part)),
    ]
    if buffer is not None:
        ins.append((buffer, None, None))
    out = ((wide, right.shape[1]), (tile, size), lambda j: (j, part))
    return call(grad_kernel, 3, ins, [out], None if buffer is None else {2: 0})[0]


CORE, X, Y = 1, 2, 4
EVEN = [(0, 1), (1, 0), (2, 3), (3, 2)]
ODD = [(1, 2), (2, 1), (0, 0), (3, 3)]


def pipelined(tokens, w_in, w_out, grad_out):
    me = lax.axis_index("row")
    edge = (me == 0) | (me == 3)
    block, hidden = tokens.shape[0], w_in.shape[1]
    near, far = 2 * block, 6 * block
    size, count = hidden // 6, 16
    order = Order()
    CALLS[0] = -1

    def across(value, bit):
        return order.send(value, "col", swap(8, bit))

    def first_hops(value):
        return across(value, CORE), across(value, X), across(value, Y), across(value, X | Y)

    def cut(part):
        return slice(part * size, (part + 1) * size)

    def half(part):
        return slice(part * 3 * size, (part + 1) * 3 * size)

    terms, sums, pres, sent = {}, {}, {}, {}
    even, odd = {}, {}
    act, dz = jnp.zeros((8 * block, hidden), BF16), jnp.zeros((8 * block, hidden), BF16)
    state = {}

    others = slice(near, near + far)

    def forward_rest(part, count):
        new = order.run(
            lambda x: product_pieces(x, others, w_in, part, count, size, False), state["x"]
        )
        for i in range(count):
            terms[2 + part + i] = new[i]

    def backward_rest(part):
        new = order.run(lambda dy: product_pieces(dy, others, w_out, part, 2, size, True), state["dy"])
        terms[8 + part], terms[9 + part] = new

    def store(target, item, value):
        if item < 2:
            return lax.dynamic_update_slice(target, unstack(value, 3), (0, item * 3 * size))
        return lax.dynamic_update_slice(target, value, (near, (item - 2) * size))

    def step(t):
        got, mid = even.pop(t - 2, None), odd.pop(t - 2, None)
        i, term = t - 4, terms.get(t)
        args, old = {}, None
        if got is not None:
            args["got"] = got
        if mid is not None:
            args["mid"], args["mine"] = mid, sums[i]
            if i >= 8:
                old = pres[i - 6 if i < 14 else i - 14]
        if term is not None:
            args["term"] = term
        if 0 <= t - 2 < count:
            args["own"] = terms[t - 2]
        if 0 <= t - 6 < count:
            args["sent"] = sent[t - 2]
        names = list(args)

        def work(*values):
            v, r = dict(zip(names, values)), {}
            if "own" in v:
                r["sum"] = v["got"] + v["own"]
            if "mid" in v:
                total = v["mine"].astype(F32) + v["mid"].astype(F32)
                if i < 8:
                    r["pre"] = total.astype(BF16)
                    out = gelu_tanh(r["pre"].astype(F32)).astype(BF16)
                else:
                    _, pullback = jax.vjp(gelu_tanh, old.astype(F32))
                    out = pullback(total)[0].astype(BF16)
                r["send"] = jnp.where(edge, v["term"], out) if "term" in v else out
            elif "term" in v:
                r["send"] = v["term"]
            return r

        r = order.run(work, *args.values())
        if "send" in r:
            sent[t] = r["send"]
            even[t] = order.send(r["send"], "row", EVEN)
        if "sum" in r:
            sums[t - 2] = r["sum"]
            odd[t] = order.send(r["sum"], "row", ODD)
        if "pre" in r:
            pres[i] = r["pre"]
        item = t - 6
        if "sent" in args:
            nonlocal act, dz
            target = act if item < 8 else dz
            where = item if item < 8 else item - 6 if item < 14 else item - 14

            def keep(value):
                return store(target, where, jnp.where(edge, got, value))

            new = order.run(keep, args["sent"])
            if item < 8:
                act = new
            else:
                dz = new

    def out_columns(part):
        state["out", part] = order.run(lambda a: product_wide(a, w_out, 2 * part, 2, size), act)

    def tokens_rest(part):
        state["tok"] = order.run(
            lambda d: product_back(
                d, slice(near, near + far), w_in, part, 3, size, state.get("tok")
            ),
            dz,
        )

    def tokens_own(part):
        state["own"] = order.run(
            lambda d: product_back(d, slice(0, near), w_in, part, 2, 2 * size, state.get("own")), dz
        )

    def add(a, b):
        return (a.astype(F32) + b.astype(F32)).astype(BF16)

    half_way = 3 * block

    def scatter_first(out_keep, tok_keep, out_got, tok_got):
        left, right = order.run(
            lambda g, h, a, b: (add(g, a), add(h, b)), out_got, tok_got, out_keep, tok_keep
        )
        to_y = across(left[block:], Y)
        to_x = across(jnp.concatenate([right[:block], right[2 * block :]]), X)
        return left[:block], right[block : 2 * block], to_y, to_x

    def scatter_second(left, right, from_y, from_x):
        over_x, over_y, mine, own = order.run(
            lambda fy, fx, a, b: (add(fy[block:], a), add(fx[block:], b), fy[:block], fx[:block]),
            from_y,
            from_x,
            left,
            right,
        )
        return mine, own, across(over_x, X), across(over_y, Y)

    def scatter_end(own, *others):
        def total(got, *rest):
            return sum((a.astype(F32) for a in rest), got.astype(F32)).astype(BF16)

        return order.run(total, *others, own)

    def swapped(values):
        return order.wait(*[across(value, CORE) for value in values])

    x_core, *x_apart = first_hops(tokens)
    terms[0], terms[1] = order.run(
        lambda b, a: product_own([a, b], w_in, 0, 2, size, False), x_core, tokens
    )
    x_apart = order.wait(*x_apart)
    x_other = swapped(x_apart)
    step(0)
    dy_core, *dy_apart = first_hops(grad_out)
    state["x"], terms[2], terms[3] = order.run(
        lambda *b: product_pieces([tokens, x_core, *x_apart, *b], others, w_in, 0, 2, size, False),
        *x_other,
    )
    step(1)
    forward_rest(2, 2)
    dy_core, *dy_apart = order.wait(dy_core, *dy_apart)
    step(2)
    dy_other = [across(dy, CORE) for dy in dy_apart]
    forward_rest(4, 1)
    step(3)
    forward_rest(5, 1)
    dy_other = order.wait(*dy_other)
    step(4)
    dy, terms[8], terms[9] = order.run(
        lambda *b: product_pieces(
            [grad_out, dy_core, *dy_apart, *b], others, w_out, 0, 2, size, True
        ),
        *dy_other,
    )
    state["dy"] = dy
    step(5)
    backward_rest(2)
    step(6)
    backward_rest(4)
    step(7)
    terms[14], terms[15] = order.run(
        lambda b, a: product_own([a, b], w_out, 0, 2, size, True), dy_core, grad_out
    )
    grad_w_out = None
    for part in range(6):
        step(8 + part)
        grad_w_out = order.run(lambda a: grad_rows(a, dy, part, 6, grad_w_out), act)
    for part in range(3):
        step(14 + part)
        out_columns(part)
    step(17)
    tokens_rest(0)
    step(18)
    tokens_rest(1)
    step(19)
    tokens_rest(2)
    out = jnp.concatenate([state["out", i] for i in range(3)], axis=1)
    tok, x = state["tok"], state["x"]
    step(20)
    step(21)
    out_got = across(out[near + half_way :], CORE)
    tok_got = across(tok[half_way:], CORE)
    parts = scatter_first(out[near : near + half_way], tok[:half_way], out_got, tok_got)
    tokens_own(0)
    tokens_own(1)
    tok_own = state["own"]
    grad_w_in = order.run(lambda d: grad_columns(x, d, 0, 2), dz)
    out_y, tok_x, out_x, tok_y = scatter_second(*parts)
    out_core = across(out[block:near], CORE)
    tok_core = across(tok_own[block:], CORE)
    grad_w_in = order.run(lambda d: grad_columns(x, d, 1, 2, grad_w_in), dz)
    out = scatter_end(out[:block], out_x, out_core, out_y)
    grad_tokens = scatter_end(tok_own[:block], tok_y, tok_core, tok_x)
    return out, grad_tokens, grad_w_in, grad_w_out


def solution(mesh):
    rows, cols = mesh.shape["row"], mesh.shape["col"]
    return jax.shard_map(
        pipelined if (rows, cols) == (4, 8) else general(rows, cols),
        mesh=mesh,
        in_specs=(P("col", "row"), P("row", "col"), P("col", "row"), P("col", "row")),
        out_specs=(P("col", "row"), P("col", "row"), P("row", "col"), P("col", "row")),
        check_vma=False,
    )
```

```python
import jax
import jax.numpy as jnp
from jax import lax
from jax.experimental import pallas as pl
from jax.experimental.pallas import tpu as pltpu
from jax.sharding import PartitionSpec as P

BF16 = jnp.bfloat16
F32 = jnp.float32


def gelu_tanh(value):
    return 0.5 * value * (1.0 + jnp.tanh(0.7978845608 * (value + 0.044715 * value * value * value)))


def dot(left, right, left_dim, right_dim, dtype=F32):
    return lax.dot_general(
        left, right, (((left_dim,), (right_dim,)), ((), ())), preferred_element_type=F32
    ).astype(dtype)


def swap(size, bit):
    return [(i, i ^ bit) for i in range(size)]


def gather_col(block, size):
    rows = block.shape[0]
    own = jnp.concatenate([block, lax.ppermute(block, "col", swap(size, 1))])
    if size == 8:
        half = rows // 2
        by_x = lax.ppermute(block, "col", swap(size, 2))
        by_y = lax.ppermute(block, "col", swap(size, 4))
        first = lax.ppermute(by_x[:half], "col", swap(size, 4))
        second = lax.ppermute(by_y[half:], "col", swap(size, 2))
        far = jnp.concatenate([by_x, by_y, first, second])
        other = lax.ppermute(far, "col", swap(size, 1))
        rest = []
        for i in range(3):
            rest += [far[i * rows : (i + 1) * rows], other[i * rows : (i + 1) * rows]]
        return own, jnp.concatenate(rest)
    rest, whole, bit = [], own, 2
    while bit < size:
        new = lax.ppermute(whole, "col", swap(size, bit))
        rest.append(new)
        whole = jnp.concatenate([whole, new])
        bit *= 2
    return own, jnp.concatenate(rest)


def scatter_col(blocks, size):
    order = [1] + [b for b in (4, 2) if b < size] + [1 << k for k in range(3, 10) if (1 << k) < size]
    keep = dict(blocks)
    for bit in order:
        send = sorted(r for r in keep if r & bit)
        stay = [r ^ bit for r in send]
        got = lax.ppermute(jnp.concatenate([keep[r] for r in send]), "col", swap(size, bit))
        rows = got.shape[0] // len(send)
        keep = {
            r: (keep[r].astype(F32) + got[i * rows : (i + 1) * rows].astype(F32)).astype(BF16)
            for i, r in enumerate(stay)
        }
    return keep[0]


def to_middle(term, size):
    mid = size // 2 - 1
    for j in range(mid):
        term = term + lax.ppermute(term, "row", [(j, j + 1), (size - 1 - j, size - 2 - j)])
    other = lax.ppermute(term, "row", [(mid, mid + 1), (mid + 1, mid)])
    return term.astype(F32) + other.astype(F32)


def from_middle(value, size, distance):
    mid = size // 2 - 1
    for j in range(mid):
        got = lax.ppermute(
            value, "row", [(mid - j, mid - j - 1), (mid + 1 + j, mid + 2 + j)]
        )
        value = jnp.where(distance == j + 1, got, value)
    return value


def general(rows_n, cols_n):
    def on_device(tokens, w_in, w_out, grad_out):
        me = lax.axis_index("row")
        mid = rows_n // 2 - 1
        distance = jnp.where(me <= mid, mid - me, me - mid - 1)
        hidden = w_in.shape[1]
        block = tokens.shape[0]
        x_own, x_rest = gather_col(tokens, cols_n)
        dy_own, dy_rest = gather_col(grad_out, cols_n)

        def cuts(parts):
            step = hidden // parts
            return [slice(i * step, (i + 1) * step) for i in range(parts)]

        own_cuts, rest_cuts = cuts(4), cuts(6)

        def forward(x, cut):
            pre = to_middle(dot(x, w_in[:, cut], 1, 0, BF16), rows_n).astype(BF16)
            act = gelu_tanh(pre.astype(F32)).astype(BF16)
            return pre, from_middle(act, rows_n, distance)

        def backward(dy, cut, pre):
            grad_act = to_middle(dot(dy, w_out[cut, :], 1, 1, BF16), rows_n)
            _, pullback = jax.vjp(gelu_tanh, pre.astype(F32))
            return from_middle(pullback(grad_act)[0].astype(BF16), rows_n, distance)

        own_f = [forward(x_own, c) for c in own_cuts]
        rest_f = [forward(x_rest, c) for c in rest_cuts]
        rest_b = [backward(dy_rest, c, f[0]) for c, f in zip(rest_cuts, rest_f)]
        own_b = [backward(dy_own, c, f[0]) for c, f in zip(own_cuts, own_f)]

        act_own = jnp.concatenate([f[1] for f in own_f], axis=1)
        act_rest = jnp.concatenate([f[1] for f in rest_f], axis=1)
        dz_rest = jnp.concatenate(rest_b, axis=1)
        dz_own = jnp.concatenate(own_b, axis=1)
        act = jnp.concatenate([act_own, act_rest])
        dz = jnp.concatenate([dz_own, dz_rest])
        x = jnp.concatenate([x_own, x_rest])
        dy = jnp.concatenate([dy_own, dy_rest])

        def split(own, rest):
            whole = {i: own[i * block : (i + 1) * block] for i in range(2)}
            for i in range(2, cols_n):
                whole[i] = rest[(i - 2) * block : (i - 1) * block]
            return whole

        out = scatter_col(
            split(dot(act_own, w_out, 1, 0, BF16), dot(act_rest, w_out, 1, 0, BF16)), cols_n
        )
        grad_tokens = scatter_col(
            split(dot(dz_own, w_in, 1, 1, BF16), dot(dz_rest, w_in, 1, 1, BF16)), cols_n
        )
        grad_w_out = dot(act, dy, 0, 0, BF16)
        grad_w_in = dot(x, dz, 0, 0, BF16)
        return out, grad_tokens, grad_w_in, grad_w_out

    return on_device


def stack(value, parts):
    return jnp.concatenate(jnp.split(value, parts, axis=1))


def unstack(value, parts):
    return jnp.concatenate(jnp.split(value, parts), axis=1)


class Order:
    def __init__(self):
        self.last = ()
        self.open = []

    def run(self, fn, *args):
        upto = [i for i, sent in enumerate(self.open) if any(sent is arg for arg in args)]
        waits = self.open[: upto[-1] + 1] if upto else []
        self.open = self.open[len(waits) :]
        first = args[0]
        held = lax.optimization_barrier((first, self.last, waits))
        done = {id(sent): value for sent, value in zip(waits, held[2])}
        self.last = fn(held[0], *[done.get(id(arg), arg) for arg in args[1:]])
        return self.last

    def wait(self, *args):
        return self.run(lambda *values: values, *args)

    def send(self, value, axis, pairs):
        value = lax.optimization_barrier((value, self.last))[0]
        got = lax.ppermute(value, axis, pairs)
        self.open.append(got)
        return got


HINTS = [10, 10, 10, 10, 10, 10, 10, 10, 10, 10, 10, 10, 10, 10, 10, 10, 10, 10, 10, 10, 10, 10, 10, 10, 10]
CALLS = [0]


def call(kernel, grid, ins, outs, alias=None, scratch=()):
    CALLS[0] += 1
    specs = [
        pl.BlockSpec(memory_space=pl.ANY) if block is None else pl.BlockSpec(block, index)
        for _, block, index in ins
    ]
    return pl.pallas_call(
        kernel,
        grid=(grid,),
        in_specs=specs,
        out_specs=[pl.BlockSpec(block, index) for _, block, index in outs],
        out_shape=[jax.ShapeDtypeStruct(shape, BF16) for shape, _, _ in outs],
        scratch_shapes=list(scratch),
        input_output_aliases=alias or {},
        compiler_params=pltpu.CompilerParams(vmem_limit_bytes=43 * 2**20),
        cost_estimate=pl.CostEstimate(flops=int(1e8 * HINTS[CALLS[0] % len(HINTS)]), bytes_accessed=1, transcendentals=0),
    )(*[array for array, _, _ in ins])


def whole(array):
    return array, array.shape, lambda j: (0, 0)


def weight_slices(weight, first, size, transposed):
    if transposed:
        return weight, (size, weight.shape[1]), lambda j: (first + j, 0)
    return weight, (weight.shape[0], size), lambda j: (0, first + j)


def product_pieces(left, rows, weight, first, pieces, size, transposed):
    dim = 1 if transposed else 0
    blocks = left if isinstance(left, list) else []

    def kernel(*refs):
        j = pl.program_id(0)
        if blocks:
            parts, w_ref, l_ref, outs = refs[: len(blocks)], *refs[len(blocks) :][:2], refs[len(blocks) + 2 :]

            @pl.when(j == 0)
            def _():
                for i, part in enumerate(parts):
                    l_ref[i * part.shape[0] : (i + 1) * part.shape[0], :] = part[...]

        else:
            l_ref, w_ref, outs = refs[0], refs[1], refs[2:]
        result = dot(l_ref[rows, :], w_ref[...], 1, dim, BF16)
        for i, out in enumerate(outs):

            @pl.when(j == i)
            def _():
                out[...] = result

    shape = (rows.stop - rows.start, size)
    outs = [(shape, shape, lambda j: (0, 0))] * pieces
    ins = [whole(array) for array in blocks or [left]]
    if blocks:
        joined = (sum(array.shape[0] for array in blocks), blocks[0].shape[1])
        outs = [(joined, joined, lambda j: (0, 0))] + outs
    return call(kernel, pieces, ins + [weight_slices(weight, first, size, transposed)], outs)


def product_own(blocks, weight, first, halves, size, transposed):
    rows, wide = sum(array.shape[0] for array in blocks), blocks[0].shape[1]

    def kernel(*refs):
        j = pl.program_id(0)
        parts, w_ref = refs[: len(blocks)], refs[len(blocks)]
        outs, joined = refs[len(blocks) + 1 : -1], refs[-1]

        @pl.when(j == 0)
        def _():
            for i, part in enumerate(parts):
                joined[i * part.shape[0] : (i + 1) * part.shape[0], :] = part[...]

        if transposed:
            result = dot(w_ref[...], joined[...], 1, 1).T.astype(BF16)
        else:
            result = dot(joined[...], w_ref[...], 1, 0, BF16)
        for i in range(3 * halves):

            @pl.when(j == i)
            def _():
                outs[i // 3][(i % 3) * rows : (i % 3 + 1) * rows, :] = result

    shape = (3 * rows, size)
    return call(
        kernel,
        3 * halves,
        [whole(array) for array in blocks] + [weight_slices(weight, first, size, transposed)],
        [(shape, shape, lambda j: (0, 0))] * halves,
        scratch=[pltpu.VMEM((rows, wide), BF16)],
    )


def product_wide(left, weight, first, tiles, size):
    def kernel(l_ref, w_ref, out):
        out[...] = dot(l_ref[...], w_ref[...], 1, 0, BF16)

    w = (weight, (weight.shape[0], size), lambda j: (0, first + j))
    out = ((left.shape[0], tiles * size), (left.shape[0], size), lambda j: (0, j))
    return call(kernel, tiles, [whole(left), w], [out])[0]


def product_back(left, rows, weight, part, parts, size, before=None):
    deep = weight.shape[1] // parts
    count = rows.stop - rows.start

    def kernel(l_ref, w_ref, *refs):
        if count <= 128:
            total = dot(w_ref[...], l_ref[rows, :], 1, 1).T
        else:
            total = dot(l_ref[rows, :], w_ref[...], 1, 1)
        if before is not None:
            total = total + refs[0][...].astype(F32)
        refs[-1][...] = total.astype(BF16)

    ins = [
        (left, (left.shape[0], deep), lambda j: (0, part)),
        (weight, (size, deep), lambda j: (j, part)),
    ]
    if before is not None:
        ins.append((before, (count, size), lambda j: (0, j)))
    out = ((count, weight.shape[0]), (count, size), lambda j: (0, j))
    return call(kernel, weight.shape[0] // size, ins, [out])[0]


def grad_kernel(left, right, *refs):
    refs[-1][...] = dot(left[...], right[...], 0, 0, BF16)


def grad_rows(left, right, part, parts, buffer=None):
    tokens, wide = left.shape
    size, tile = wide // parts, right.shape[1] // 3
    ins = [
        (left, (tokens, size), lambda j: (0, part)),
        (right, (tokens, tile), lambda j: (0, j)),
    ]
    if buffer is not None:
        ins.append((buffer, None, None))
    out = ((wide, right.shape[1]), (size, tile), lambda j: (part, j))
    return call(grad_kernel, 3, ins, [out], None if buffer is None else {2: 0})[0]


def grad_columns(left, right, part, parts, buffer=None):
    tokens, wide = left.shape
    size, tile = right.shape[1] // parts, wide // 3
    ins = [
        (left, (tokens, tile), lambda j: (0, j)),
        (right, (tokens, size), lambda j: (0, part)),
    ]
    if buffer is not None:
        ins.append((buffer, None, None))
    out = ((wide, right.shape[1]), (tile, size), lambda j: (j, part))
    return call(grad_kernel, 3, ins, [out], None if buffer is None else {2: 0})[0]


CORE, X, Y = 1, 2, 4
EVEN = [(0, 1), (1, 0), (2, 3), (3, 2)]
ODD = [(1, 2), (2, 1), (0, 0), (3, 3)]


def pipelined(tokens, w_in, w_out, grad_out):
    me = lax.axis_index("row")
    edge = (me == 0) | (me == 3)
    block, hidden = tokens.shape[0], w_in.shape[1]
    near, far = 2 * block, 6 * block
    size, count = hidden // 6, 16
    order = Order()
    CALLS[0] = -1

    def across(value, bit):
        return order.send(value, "col", swap(8, bit))

    def first_hops(value):
        return across(value, CORE), across(value, X), across(value, Y), across(value, X | Y)

    def cut(part):
        return slice(part * size, (part + 1) * size)

    def half(part):
        return slice(part * 3 * size, (part + 1) * 3 * size)

    terms, sums, pres, sent = {}, {}, {}, {}
    even, odd = {}, {}
    act, dz = jnp.zeros((8 * block, hidden), BF16), jnp.zeros((8 * block, hidden), BF16)
    state = {}

    others = slice(near, near + far)

    def forward_rest(part, count):
        new = order.run(
            lambda x: product_pieces(x, others, w_in, part, count, size, False), state["x"]
        )
        for i in range(count):
            terms[2 + part + i] = new[i]

    def backward_rest(part):
        new = order.run(lambda dy: product_pieces(dy, others, w_out, part, 2, size, True), state["dy"])
        terms[8 + part], terms[9 + part] = new

    def store(target, item, value):
        if item < 2:
            return lax.dynamic_update_slice(target, unstack(value, 3), (0, item * 3 * size))
        return lax.dynamic_update_slice(target, value, (near, (item - 2) * size))

    def step(t):
        got, mid = even.pop(t - 2, None), odd.pop(t - 2, None)
        i, term = t - 4, terms.get(t)
        args, old = {}, None
        if got is not None:
            args["got"] = got
        if mid is not None:
            args["mid"], args["mine"] = mid, sums[i]
            if i >= 8:
                old = pres[i - 6 if i < 14 else i - 14]
        if term is not None:
            args["term"] = term
        if 0 <= t - 2 < count:
            args["own"] = terms[t - 2]
        if 0 <= t - 6 < count:
            args["sent"] = sent[t - 2]
        names = list(args)

        def work(*values):
            v, r = dict(zip(names, values)), {}
            if "own" in v:
                r["sum"] = v["got"] + v["own"]
            if "mid" in v:
                total = v["mine"].astype(F32) + v["mid"].astype(F32)
                if i < 8:
                    r["pre"] = total.astype(BF16)
                    out = gelu_tanh(r["pre"].astype(F32)).astype(BF16)
                else:
                    _, pullback = jax.vjp(gelu_tanh, old.astype(F32))
                    out = pullback(total)[0].astype(BF16)
                r["send"] = jnp.where(edge, v["term"], out) if "term" in v else out
            elif "term" in v:
                r["send"] = v["term"]
            return r

        r = order.run(work, *args.values())
        if "send" in r:
            sent[t] = r["send"]
            even[t] = order.send(r["send"], "row", EVEN)
        if "sum" in r:
            sums[t - 2] = r["sum"]
            odd[t] = order.send(r["sum"], "row", ODD)
        if "pre" in r:
            pres[i] = r["pre"]
        item = t - 6
        if "sent" in args:
            nonlocal act, dz
            target = act if item < 8 else dz
            where = item if item < 8 else item - 6 if item < 14 else item - 14

            def keep(value):
                return store(target, where, jnp.where(edge, got, value))

            new = order.run(keep, args["sent"])
            if item < 8:
                act = new
            else:
                dz = new

    def out_columns(part):
        state["out", part] = order.run(lambda a: product_wide(a, w_out, 2 * part, 2, size), act)

    def tokens_rest(part):
        state["tok"] = order.run(
            lambda d: product_back(
                d, slice(near, near + far), w_in, part, 3, size, state.get("tok")
            ),
            dz,
        )

    def tokens_own(part):
        state["own"] = order.run(
            lambda d: product_back(d, slice(0, near), w_in, part, 2, 2 * size, state.get("own")), dz
        )

    def add(a, b):
        return (a.astype(F32) + b.astype(F32)).astype(BF16)

    half_way = 3 * block

    def scatter_first(out_keep, tok_keep, out_got, tok_got):
        left, right = order.run(
            lambda g, h, a, b: (add(g, a), add(h, b)), out_got, tok_got, out_keep, tok_keep
        )
        to_y = across(left[block:], Y)
        to_x = across(jnp.concatenate([right[:block], right[2 * block :]]), X)
        return left[:block], right[block : 2 * block], to_y, to_x

    def scatter_second(left, right, from_y, from_x):
        over_x, over_y, mine, own = order.run(
            lambda fy, fx, a, b: (add(fy[block:], a), add(fx[block:], b), fy[:block], fx[:block]),
            from_y,
            from_x,
            left,
            right,
        )
        return mine, own, across(over_x, X), across(over_y, Y)

    def scatter_end(own, *others):
        def total(got, *rest):
            return sum((a.astype(F32) for a in rest), got.astype(F32)).astype(BF16)

        return order.run(total, *others, own)

    def swapped(values):
        return order.wait(*[across(value, CORE) for value in values])

    x_core, *x_apart = first_hops(tokens)
    terms[0], terms[1] = order.run(
        lambda b, a: product_own([a, b], w_in, 0, 2, size, False), x_core, tokens
    )
    x_apart = order.wait(*x_apart)
    x_other = swapped(x_apart)
    step(0)
    dy_core, *dy_apart = first_hops(grad_out)
    state["x"], terms[2], terms[3] = order.run(
        lambda *b: product_pieces([tokens, x_core, *x_apart, *b], others, w_in, 0, 2, size, False),
        *x_other,
    )
    step(1)
    forward_rest(2, 2)
    dy_core, *dy_apart = order.wait(dy_core, *dy_apart)
    step(2)
    dy_other = [across(dy, CORE) for dy in dy_apart]
    forward_rest(4, 1)
    step(3)
    forward_rest(5, 1)
    dy_other = order.wait(*dy_other)
    step(4)
    dy, terms[8], terms[9] = order.run(
        lambda *b: product_pieces(
            [grad_out, dy_core, *dy_apart, *b], others, w_out, 0, 2, size, True
        ),
        *dy_other,
    )
    state["dy"] = dy
    step(5)
    backward_rest(2)
    step(6)
    backward_rest(4)
    step(7)
    terms[14], terms[15] = order.run(
        lambda b, a: product_own([a, b], w_out, 0, 2, size, True), dy_core, grad_out
    )
    grad_w_out = None
    for part in range(6):
        step(8 + part)
        grad_w_out = order.run(lambda a: grad_rows(a, dy, part, 6, grad_w_out), act)
    for part in range(3):
        step(14 + part)
        out_columns(part)
    step(17)
    tokens_rest(0)
    step(18)
    tokens_rest(1)
    step(19)
    tokens_rest(2)
    out = jnp.concatenate([state["out", i] for i in range(3)], axis=1)
    tok, x = state["tok"], state["x"]
    step(20)
    tokens_own(0)
    step(21)
    out_got = across(out[near + half_way :], CORE)
    tok_got = across(tok[half_way:], CORE)
    parts = scatter_first(out[near : near + half_way], tok[:half_way], out_got, tok_got)
    tokens_own(1)
    tok_own = state["own"]
    grad_w_in = order.run(lambda d: grad_columns(x, d, 0, 2), dz)
    out_y, tok_x, out_x, tok_y = scatter_second(*parts)
    out_core = across(out[block:near], CORE)
    tok_core = across(tok_own[block:], CORE)
    grad_w_in = order.run(lambda d: grad_columns(x, d, 1, 2, grad_w_in), dz)
    out = scatter_end(out[:block], out_x, out_core, out_y)
    grad_tokens = scatter_end(tok_own[:block], tok_y, tok_core, tok_x)
    return out, grad_tokens, grad_w_in, grad_w_out


def solution(mesh):
    rows, cols = mesh.shape["row"], mesh.shape["col"]
    return jax.shard_map(
        pipelined if (rows, cols) == (4, 8) else general(rows, cols),
        mesh=mesh,
        in_specs=(P("col", "row"), P("row", "col"), P("col", "row"), P("col", "row")),
        out_specs=(P("col", "row"), P("col", "row"), P("row", "col"), P("col", "row")),
        check_vma=False,
    )
```
